512 devices in a mesh: basis: 32 (over y, z_hi, core), ex: 16 (over z_lo, x).
Axes of the slice: x: 4, y: 8, z: 8 (z_hi: 2, z_lo: 4; z = z_hi * 4 + z_lo), core: 2. Of those that a mesh axis runs over, the one named last changes fastest.
Arguments:
- grad_out: bfloat16 [768, 13824], P('ex', 'basis'), may hold values from -6 to 6
- acts: bfloat16 [768, 5120], P('basis', 'ex'), may hold values from -6 to 6
- basis_out: bfloat16 [13824, 13824], P('basis', 'ex'), may hold values from -0.0546875 to 0.0546875
- basis_in: bfloat16 [5120, 5120], P('ex', 'basis'), may hold values from -0.078125 to 0.078125
- eigvals: float32 [13824, 5120], P('ex', 'basis'), may hold values from 0.1 to 10
- counts: int32 [48], replicated, may hold values from 1 to 16, as said below
Outputs:
- scores: float32 [16, 32], replicated
The draws below stay inside these ranges and needn't reach their ends.
Inputs may be any that keep to these rules, and one draw needn't show every extreme that they name: `counts`: every draw holds some example with exactly 16 tokens in use.
All inputs are finite; a program needn't handle non-finite values.
Results may differ from the reference program's by a relative error of at most 0.0055.
Values may be sent and summed in bfloat16 or wider, within the bound.
No kernel may reach another device: no remote copies, remote signals or barrier semaphores. Data moves between devices by JAX's collectives and lax.ppermute only.
A program may use at most 64 MiB of HBM per device.

```python
import math
import jax
import jax.numpy as jnp
from jax import lax

D = 5120
FF = 13824
NQ = 16
NT = 32
TOKX = 16
NTOK = 768


def draw_counts(key, part):
    key = jax.random.fold_in(key, 7)
    first, second = jax.random.split(key)
    values = jax.random.randint(first, (NQ + NT,), 1, TOKX + 1)
    picked = jax.random.randint(second, (), 0, NQ + NT)
    return jnp.where(jnp.arange(NQ + NT) == picked, TOKX, values).astype(jnp.int32)


def block_levels(own_key, dims, cuts, least, largest):
    factor_of, own = 1.0, jax.random.fold_in(own_key, 6)
    for position, shards_of in cuts:
        heights = jnp.exp(jax.random.uniform(jax.random.fold_in(own, position), (shards_of,), jnp.float32, least / len(cuts), largest / len(cuts)))
        factor_of = factor_of * jnp.repeat(heights, dims[position] // shards_of).reshape([-1 if axis == position else 1 for axis in range(len(dims))])
    return factor_of


def noise(key, shape, spread, limit, cuts=(), kind=jnp.bfloat16):
    array = spread * jax.random.normal(key, shape, jnp.float32)
    if cuts:
        array = array * block_levels(key, shape, cuts, -0.22, 0.18)
    return jnp.clip(array, -limit, limit).astype(kind)


def setup_inputs(seed: int = 0) -> dict:
    arg_keys = jax.random.split(jax.random.key(seed), 7)
    grad_out = noise(arg_keys[0], (NTOK, FF), 1.0, 6.0, ((0, 16), (1, 32)))
    acts = noise(arg_keys[1], (NTOK, D), 1.0, 6.0, ((0, 32), (1, 16)))
    basis_out = noise(arg_keys[2], (FF, FF), FF ** -0.5, 0.0546875, ((0, 32), (1, 16)))
    basis_in = noise(arg_keys[3], (D, D), D ** -0.5, 0.078125, ((0, 16), (1, 32)))
    eigvals = jnp.clip(jnp.exp(math.log(10.0) - 4.6051702 * jax.random.uniform(arg_keys[4], (FF, D), jnp.float32) ** block_levels(arg_keys[4], (FF, D), ((0, 16), (1, 32)), -0.2, 0.2)), 0.1, 10.0)
    counts = draw_counts(jax.random.fold_in(arg_keys[6], 71), 0)
    return {"grad_out": grad_out, "acts": acts, "basis_out": basis_out, "basis_in": basis_in, "eigvals": eigvals, "counts": counts}


def reference(grad_out, acts, basis_out, basis_in, eigvals, counts):
    slots = jnp.arange(NTOK, dtype=jnp.int32)
    mask = (slots % TOKX < jnp.repeat(counts, TOKX)).astype(jnp.float32)
    rot_grad = (jnp.dot(grad_out, basis_out, preferred_element_type=jnp.float32) * mask[:, None]).astype(jnp.bfloat16)
    rot_act = jnp.dot(acts, basis_in, preferred_element_type=jnp.float32).astype(jnp.bfloat16)
    query_grad = rot_grad[:NQ * TOKX].reshape(NQ, TOKX, FF)
    query_act = rot_act[:NQ * TOKX].reshape(NQ, TOKX, D)
    train_grad = rot_grad[NQ * TOKX:]
    train_act = rot_act[NQ * TOKX:]

    def one_query(pair):
        grad_q, act_q = pair
        outer = jnp.dot(grad_q.T, act_q, preferred_element_type=jnp.float32)
        precond = (outer / eigvals).astype(jnp.bfloat16)
        projected = lax.dot_general(train_act, precond, (((1,), (1,)), ((), ())), preferred_element_type=jnp.float32)
        return lax.optimization_barrier(jnp.sum((projected * train_grad).reshape(NT, TOKX * FF), axis=1))
    raw = lax.map(one_query, (query_grad, query_act))
    return raw / (TOKX * jnp.sqrt(jnp.float32(FF) * jnp.float32(D)))
```

```python
import jax
import jax.numpy as jnp
from jax import lax
from jax.sharding import Mesh, PartitionSpec as P

D = 5120
FF = 13824
NQ = 16
NT = 32
TOKX = 16
NTOK = 768

SIZES = (8, 2, 2, 4, 4)
NAMES = ("y", "zh", "core", "zl", "x")
BASIS = ("y", "zh", "core")
EX = ("zl", "x")
SWAP = ((0, 1), (1, 0))
bf16 = jnp.bfloat16
f32 = jnp.float32


def spread(x, axes, n):
    return lax.all_to_all(
        jnp.broadcast_to(x[None], (n,) + x.shape), axes, 0, 0, tiled=True
    )


def swap(x, axis):
    return lax.ppermute(x, axis, SWAP)


def ordered(mine, other, second, axis):
    lo = jnp.where(second, other, mine)
    hi = jnp.where(second, mine, other)
    return lo, hi


def body(grad_out, acts, basis_out, basis_in, eigvals, counts):
    core = lax.axis_index("core")
    second = core == 1
    half = basis_out.shape[1] // 2

    grads = spread(grad_out, EX, 16).reshape(NTOK, -1)

    w_lo, w_hi = basis_out[:, :half], basis_out[:, half:]
    w_mine = jnp.where(second, w_hi, w_lo)
    w_other = swap(jnp.where(second, w_lo, w_hi), "core")
    eig_t = eigvals.T
    e_lo, e_hi = eig_t[:, :half], eig_t[:, half:]
    e_mine = jnp.where(second, e_hi, e_lo)
    e_other = swap(jnp.where(second, e_lo, e_hi), "core")
    eig = jnp.concatenate(ordered(e_mine, e_other, second, 0), axis=0)
    recip = 1.0 / eig

    b_other = swap(basis_in, "core")
    b_in = jnp.concatenate(ordered(basis_in, b_other, second, 1), axis=1)
    act = spread(acts, ("y", "zh"), 16).reshape(NTOK // 2, -1)
    part_act = jnp.dot(act, b_in, preferred_element_type=f32)
    part_act = lax.all_to_all(
        part_act.reshape(16, 24, -1), EX, 0, 0, tiled=True
    )
    act_piece = jnp.sum(part_act, axis=0).astype(bf16)
    act_half = spread(act_piece, EX, 16)
    act_other = swap(act_half, "core")
    rot_act = jnp.stack(
        ordered(
            act_half.reshape(16, 24, -1), act_other.reshape(16, 24, -1), second, 0
        ),
        axis=1,
    ).reshape(NTOK, -1)

    g_other = swap(grads, "core")
    partial = jnp.dot(grads, w_mine, preferred_element_type=f32) + jnp.dot(
        g_other, w_other, preferred_element_type=f32
    )
    rows = NTOK // 8
    pieces = lax.all_to_all(
        partial.astype(bf16).reshape(8, rows, -1), "y", 0, 0, tiled=True
    )
    piece = jnp.sum(pieces.astype(f32), axis=0)
    piece = piece + swap(piece, "zh")
    slots = lax.axis_index("y") * rows + jnp.arange(rows, dtype=jnp.int32)
    used = slots % TOKX < jnp.take(counts, slots // TOKX)
    piece = (piece * used.astype(f32)[:, None]).astype(bf16)
    rot_grad = spread(piece, "y", 8).reshape(NTOK, -1)

    cols_grad = rot_grad.shape[1]
    cols_act = rot_act.shape[1]
    query_grad = rot_grad[: NQ * TOKX].reshape(NQ, TOKX, cols_grad)
    query_act = rot_act[: NQ * TOKX].reshape(NQ, TOKX, cols_act)
    train_grad = rot_grad[NQ * TOKX :]
    train_act = rot_act[NQ * TOKX :]

    def one_query(pair):
        grad_q, act_q = pair
        outer = lax.dot_general(
            act_q, grad_q, (((0,), (0,)), ((), ())), preferred_element_type=f32
        )
        precond = (outer * recip).astype(bf16)
        projected = jnp.dot(train_act, precond, preferred_element_type=f32)
        return jnp.sum((projected * train_grad).reshape(NT, TOKX * cols_grad), axis=1)

    raw = lax.map(one_query, (query_grad, query_act))
    scaled = raw / (TOKX * jnp.sqrt(f32(FF) * f32(D)))
    flat = scaled.reshape(4, 128)
    flat = jnp.sum(spread(flat, ("core",) + EX, 32), axis=0)
    flat = jnp.sum(spread(flat, ("y", "zh"), 16), axis=0)
    return flat.reshape(NQ, NT)


def solution(mesh):
    fine = Mesh(mesh.devices.reshape(SIZES), NAMES)
    return jax.shard_map(
        body,
        mesh=fine,
        in_specs=(
            P(EX, BASIS),
            P(BASIS, EX),
            P(BASIS, EX),
            P(EX, BASIS),
            P(EX, BASIS),
            P(),
        ),
        out_specs=P(),
        check_vma=False,
    )
```

```python
import jax
import jax.numpy as jnp
from jax import lax
from jax.sharding import Mesh, PartitionSpec as P

D = 5120
FF = 13824
NQ = 16
NT = 32
TOKX = 16
NTOK = 768

SIZES = (8, 2, 2, 4, 4)
NAMES = ("y", "zh", "core", "zl", "x")
BASIS = ("y", "zh", "core")
EX = ("zl", "x")
SWAP = ((0, 1), (1, 0))
bf16 = jnp.bfloat16
f32 = jnp.float32


def spread(x, axes, n):
    return lax.all_to_all(
        jnp.broadcast_to(x[None], (n,) + x.shape), axes, 0, 0, tiled=True
    )


def swap(x, axis):
    return lax.ppermute(x, axis, SWAP)


def tie(*values):
    return lax.optimization_barrier(values)


def ordered(mine, other, second):
    lo = jnp.where(second, other, mine)
    hi = jnp.where(second, mine, other)
    return lo, hi


def body(grad_out, acts, basis_out, basis_in, eigvals, counts):
    core = lax.axis_index("core")
    second = core == 1
    half = basis_out.shape[1] // 2

    act = spread(acts, ("y", "zh"), 16)
    grads = lax.all_gather(grad_out, "x", axis=0, tiled=True)

    w_lo, w_hi = basis_out[:, :half], basis_out[:, half:]
    w_mine = jnp.where(second, w_hi, w_lo)
    w_other = swap(jnp.where(second, w_lo, w_hi), "core")
    b_other = swap(basis_in, "core")
    grads, act, w_other, b_other = tie(grads, act, w_other, b_other)

    b_in = jnp.concatenate(ordered(basis_in, b_other, second), axis=1)
    part_act = jnp.dot(
        act.reshape(NTOK // 2, -1), b_in, preferred_element_type=f32
    )
    grads, part_act = tie(grads, part_act)
    parts = lax.all_to_all(part_act.reshape(16, 24, -1), EX, 0, 0, tiled=True)
    grads = lax.all_gather(grads, "zl", axis=0, tiled=True)
    grads, parts = tie(grads, parts)
    g_other = swap(grads, "core")
    partial = jnp.dot(grads, w_mine, preferred_element_type=f32) + jnp.dot(
        g_other, w_other, preferred_element_type=f32
    )
    partial = partial.astype(bf16)

    rows = NTOK // 8
    pieces = lax.all_to_all(
        partial.reshape(8, rows, -1), "y", 0, 0, tiled=True
    )
    partial, act_piece = tie(partial, jnp.sum(parts, axis=0).astype(bf16))
    act_x = lax.all_gather(act_piece, "x", axis=0, tiled=True)
    pieces, act_x = tie(pieces, act_x)

    piece = jnp.sum(pieces.astype(f32), axis=0)
    piece_other = swap(piece, "zh")
    act_half = lax.all_gather(act_x, "zl", axis=0, tiled=True)
    slots = lax.axis_index("y") * rows + jnp.arange(rows, dtype=jnp.int32)
    used = slots % TOKX < jnp.take(counts, slots // TOKX)
    piece = ((piece + piece_other) * used.astype(f32)[:, None]).astype(bf16)
    piece, act_half = tie(piece, act_half)

    rot_grad = spread(piece, "y", 8).reshape(NTOK, -1)
    act_other = swap(act_half, "core")
    rot_act = jnp.stack(
        ordered(act_half.reshape(16, 24, -1), act_other.reshape(16, 24, -1), second),
        axis=1,
    ).reshape(NTOK, -1)
    eig_t = eigvals.T
    e_lo, e_hi = eig_t[:, :half], eig_t[:, half:]
    e_mine = jnp.where(second, e_hi, e_lo)
    e_other = swap(jnp.where(second, e_lo, e_hi), "core")
    recip = 1.0 / jnp.concatenate(ordered(e_mine, e_other, second), axis=0)

    cols_grad = rot_grad.shape[1]
    cols_act = rot_act.shape[1]
    query_grad = rot_grad[: NQ * TOKX].reshape(NQ, TOKX, cols_grad)
    query_act = rot_act[: NQ * TOKX].reshape(NQ, TOKX, cols_act)
    train_grad = rot_grad[NQ * TOKX :]
    train_act = rot_act[NQ * TOKX :]

    def one_query(pair):
        grad_q, act_q = pair
        outer = lax.dot_general(
            act_q, grad_q, (((0,), (0,)), ((), ())), preferred_element_type=f32
        )
        precond = (outer * recip).astype(bf16)
        projected = jnp.dot(train_act, precond, preferred_element_type=f32)
        return jnp.sum((projected * train_grad).reshape(NT, TOKX * cols_grad), axis=1)

    raw = lax.map(one_query, (query_grad, query_act))
    scaled = raw / (TOKX * jnp.sqrt(f32(FF) * f32(D)))
    flat = scaled.reshape(4, 128)
    flat = jnp.sum(spread(flat, ("core",) + EX, 32), axis=0)
    flat = jnp.sum(spread(flat, ("y", "zh"), 16), axis=0)
    return flat.reshape(NQ, NT)


def solution(mesh):
    fine = Mesh(mesh.devices.reshape(SIZES), NAMES)
    return jax.shard_map(
        body,
        mesh=fine,
        in_specs=(
            P(EX, BASIS),
            P(BASIS, EX),
            P(BASIS, EX),
            P(EX, BASIS),
            P(EX, BASIS),
            P(),
        ),
        out_specs=P(),
        check_vma=False,
    )
```

```python
import jax
import jax.numpy as jnp
from jax import lax
from jax.sharding import Mesh, PartitionSpec as P

D = 5120
FF = 13824
NQ = 16
NT = 32
TOKX = 16
NTOK = 768

SIZES = (8, 2, 2, 4, 4)
NAMES = ("y", "zh", "core", "zl", "x")
BASIS = ("y", "zh", "core")
EX = ("zl", "x")
SWAP = ((0, 1), (1, 0))
bf16 = jnp.bfloat16
f32 = jnp.float32


def spread(x, axes, n):
    return lax.all_to_all(
        jnp.broadcast_to(x[None], (n,) + x.shape), axes, 0, 0, tiled=True
    )


def swap(x, axis):
    return lax.ppermute(x, axis, SWAP)


def tie(*values):
    return lax.optimization_barrier(values)


def ordered(mine, other, second):
    lo = jnp.where(second, other, mine)
    hi = jnp.where(second, mine, other)
    return lo, hi


def doubled(x, axis, bit):
    n = SIZES[NAMES.index(axis)]
    other = lax.ppermute(x, axis, [(i, i ^ bit) for i in range(n)])
    second = lax.axis_index(axis) // bit % 2 == 1
    return jnp.concatenate(ordered(x, other, second), axis=0)


def scattered(x, axis, dim):
    here = lax.axis_index(axis)
    total = lax.dynamic_index_in_dim(x, here, dim, keepdims=False)
    for bit in (1, 2, 3):
        block = lax.dynamic_index_in_dim(x, here ^ bit, dim, keepdims=False)
        total = total + lax.ppermute(block, axis, [(i, i ^ bit) for i in range(4)])
    return total


def body(grad_out, acts, basis_out, basis_in, eigvals, counts):
    core = lax.axis_index("core")
    second = core == 1
    half = basis_out.shape[1] // 2

    grads = spread(grad_out, EX, 16).reshape(NTOK, -1)
    act = doubled(acts, "zh", 1)
    w_lo, w_hi = basis_out[:, :half], basis_out[:, half:]
    w_mine = jnp.where(second, w_hi, w_lo)
    w_other = swap(jnp.where(second, w_lo, w_hi), "core")
    b_other = swap(basis_in, "core")
    b_in = jnp.concatenate(ordered(basis_in, b_other, second), axis=1)
    act = doubled(act, "y", 1)
    act = doubled(act, "y", 2)
    grads, w_other, act = tie(grads, w_other, act)

    g_other = swap(grads, "core")
    act = doubled(act, "y", 4)
    partial = jnp.dot(grads, w_mine, preferred_element_type=f32) + jnp.dot(
        g_other, w_other, preferred_element_type=f32
    )
    partial, act, b_in = tie(partial.astype(bf16), act, b_in)

    rows = NTOK // 8
    pieces = lax.all_to_all(
        partial.reshape(8, rows, -1), "y", 0, 0, tiled=True
    )
    part_act = jnp.dot(act, b_in, preferred_element_type=f32)
    part_act = part_act.reshape(4, 4, 24, -1)
    part_act = scattered(part_act, "x", 1)
    act_piece = scattered(part_act, "zl", 0).astype(bf16)
    pieces, act_piece = tie(pieces, act_piece)

    piece = jnp.sum(pieces.astype(f32), axis=0)
    piece_other = swap(piece, "zh")
    act_x = lax.all_gather(act_piece, "x", axis=0, tiled=True)
    slots = lax.axis_index("y") * rows + jnp.arange(rows, dtype=jnp.int32)
    used = slots % TOKX < jnp.take(counts, slots // TOKX)
    piece = ((piece + piece_other) * used.astype(f32)[:, None]).astype(bf16)
    piece, act_x = tie(piece, act_x)

    rot_grad = spread(piece, "y", 8).reshape(NTOK, -1)
    act_half = lax.all_gather(act_x, "zl", axis=0, tiled=True)
    act_other = swap(act_half, "core")
    rot_act = jnp.stack(
        ordered(act_half.reshape(16, 24, -1), act_other.reshape(16, 24, -1), second),
        axis=1,
    ).reshape(NTOK, -1)
    eig_t = eigvals.T
    e_lo, e_hi = eig_t[:, :half], eig_t[:, half:]
    e_mine = jnp.where(second, e_hi, e_lo)
    e_other = swap(jnp.where(second, e_lo, e_hi), "core")
    recip = 1.0 / jnp.concatenate(ordered(e_mine, e_other, second), axis=0)

    cols_grad = rot_grad.shape[1]
    cols_act = rot_act.shape[1]
    query_grad = rot_grad[: NQ * TOKX].reshape(NQ, TOKX, cols_grad)
    query_act = rot_act[: NQ * TOKX].reshape(NQ, TOKX, cols_act)
    train_grad = rot_grad[NQ * TOKX :]
    train_act = rot_act[NQ * TOKX :]

    def one_query(pair):
        grad_q, act_q = pair
        outer = lax.dot_general(
            act_q, grad_q, (((0,), (0,)), ((), ())), preferred_element_type=f32
        )
        precond = (outer * recip).astype(bf16)
        projected = jnp.dot(train_act, precond, preferred_element_type=f32)
        return jnp.sum((projected * train_grad).reshape(NT, TOKX * cols_grad), axis=1)

    raw = lax.map(one_query, (query_grad, query_act))
    scaled = raw / (TOKX * jnp.sqrt(f32(FF) * f32(D)))
    flat = scaled.reshape(4, 128)
    flat = jnp.sum(spread(flat, ("core",) + EX, 32), axis=0)
    flat = jnp.sum(spread(flat, ("y", "zh"), 16), axis=0)
    return flat.reshape(NQ, NT)


def solution(mesh):
    fine = Mesh(mesh.devices.reshape(SIZES), NAMES)
    return jax.shard_map(
        body,
        mesh=fine,
        in_specs=(
            P(EX, BASIS),
            P(BASIS, EX),
            P(BASIS, EX),
            P(EX, BASIS),
            P(EX, BASIS),
            P(),
        ),
        out_specs=P(),
        check_vma=False,
    )
```

```python
import jax
import jax.numpy as jnp
from jax import lax
from jax.sharding import Mesh, PartitionSpec as P

D = 5120
FF = 13824
NQ = 16
NT = 32
TOKX = 16
NTOK = 768

SIZES = (8, 2, 2, 4, 4)
NAMES = ("y", "zh", "core", "zl", "x")
BASIS = ("y", "zh", "core")
EX = ("zl", "x")
SWAP = ((0, 1), (1, 0))
bf16 = jnp.bfloat16
f32 = jnp.float32


def spread(x, axes, n):
    return lax.all_to_all(
        jnp.broadcast_to(x[None], (n,) + x.shape), axes, 0, 0, tiled=True
    )


def swap(x, axis):
    return lax.ppermute(x, axis, SWAP)


def tie(*values):
    return lax.optimization_barrier(values)


def ordered(mine, other, second):
    lo = jnp.where(second, other, mine)
    hi = jnp.where(second, mine, other)
    return lo, hi


def doubled(x, axis, bit):
    n = SIZES[NAMES.index(axis)]
    other = lax.ppermute(x, axis, [(i, i ^ bit) for i in range(n)])
    second = lax.axis_index(axis) // bit % 2 == 1
    return jnp.concatenate(ordered(x, other, second), axis=0)


def scattered(x, axis, dim):
    here = lax.axis_index(axis)
    total = lax.dynamic_index_in_dim(x, here, dim, keepdims=False)
    for bit in (1, 2, 3):
        block = lax.dynamic_index_in_dim(x, here ^ bit, dim, keepdims=False)
        total = total + lax.ppermute(block, axis, [(i, i ^ bit) for i in range(4)])
    return total


def summed(x, axis):
    one, two, three = (
        lax.ppermute(x, axis, [(i, i ^ bit) for i in range(4)]) for bit in (1, 2, 3)
    )
    return (x + one) + (two + three)


def body(grad_out, acts, basis_out, basis_in, eigvals, counts):
    core = lax.axis_index("core")
    second = core == 1
    half = basis_out.shape[1] // 2

    grads = spread(grad_out, EX, 16).reshape(NTOK, -1)
    act = doubled(acts, "zh", 1)
    w_lo, w_hi = basis_out[:, :half], basis_out[:, half:]
    w_mine = jnp.where(second, w_hi, w_lo)
    w_other = swap(jnp.where(second, w_lo, w_hi), "core")
    b_other = swap(basis_in, "core")
    b_in = jnp.concatenate(ordered(basis_in, b_other, second), axis=1)
    act = doubled(act, "y", 1)
    act = doubled(act, "y", 2)
    grads, w_other, b_in, act = tie(grads, w_other, b_in, act)

    g_other = swap(grads, "core")
    partial = jnp.dot(grads, w_mine, preferred_element_type=f32)
    g_other, partial = tie(g_other, partial)
    partial = partial + jnp.dot(g_other, w_other, preferred_element_type=f32)
    partial, act = tie(partial.astype(bf16), act)

    rows = NTOK // 8
    pieces = lax.all_to_all(
        partial.reshape(8, rows, -1), "y", 0, 0, tiled=True
    )
    act = doubled(act, "y", 4)
    part_act = jnp.dot(act, b_in, preferred_element_type=f32)
    part_act = scattered(part_act.reshape(4, 4, 24, -1), "x", 1)
    eig_t = eigvals.T
    e_lo, e_hi = eig_t[:, :half], eig_t[:, half:]
    e_mine = jnp.where(second, e_hi, e_lo)
    e_other = swap(jnp.where(second, e_lo, e_hi), "core")
    slots = lax.axis_index("y") * rows + jnp.arange(rows, dtype=jnp.int32)
    used = slots % TOKX < jnp.take(counts, slots // TOKX)
    used = used.astype(f32)[:, None]
    pieces, part_act, used, e_other = tie(pieces, part_act, used, e_other)

    piece = jnp.sum(pieces.astype(f32), axis=0)
    piece_other = swap(piece, "zh")
    act_piece = summed(part_act, "zl").astype(bf16)
    piece = ((piece + piece_other) * used).astype(bf16)

    rot_grad = spread(piece, "y", 8).reshape(NTOK, -1)
    act_half = lax.all_gather(act_piece, "x", axis=0)
    act_half = jnp.swapaxes(act_half, 0, 1).reshape(16, 24, -1)
    act_other = swap(act_half, "core")
    rot_act = jnp.stack(ordered(act_half, act_other, second), axis=1).reshape(NTOK, -1)
    recip = 1.0 / jnp.concatenate(ordered(e_mine, e_other, second), axis=0)

    cols_grad = rot_grad.shape[1]
    cols_act = rot_act.shape[1]
    query_grad = rot_grad[: NQ * TOKX].reshape(NQ, TOKX, cols_grad)
    query_act = rot_act[: NQ * TOKX].reshape(NQ, TOKX, cols_act)
    train_grad = rot_grad[NQ * TOKX :]
    train_act = rot_act[NQ * TOKX :]

    def one_query(pair):
        grad_q, act_q = pair
        outer = lax.dot_general(
            act_q, grad_q, (((0,), (0,)), ((), ())), preferred_element_type=f32
        )
        precond = (outer * recip).astype(bf16)
        projected = jnp.dot(train_act, precond, preferred_element_type=f32)
        return jnp.sum((projected * train_grad).reshape(NT, TOKX * cols_grad), axis=1)

    raw = lax.map(one_query, (query_grad, query_act))
    scaled = raw / (TOKX * jnp.sqrt(f32(FF) * f32(D)))
    flat = scaled.reshape(4, 128)
    flat = jnp.sum(spread(flat, ("core",) + EX, 32), axis=0)
    flat = jnp.sum(spread(flat, ("y", "zh"), 16), axis=0)
    return flat.reshape(NQ, NT)


def solution(mesh):
    fine = Mesh(mesh.devices.reshape(SIZES), NAMES)
    return jax.shard_map(
        body,
        mesh=fine,
        in_specs=(
            P(EX, BASIS),
            P(BASIS, EX),
            P(BASIS, EX),
            P(EX, BASIS),
            P(EX, BASIS),
            P(),
        ),
        out_specs=P(),
        check_vma=False,
    )
```

```python
import jax
import jax.numpy as jnp
from jax import lax
from jax.experimental import pallas as pl
from jax.experimental.pallas import tpu as pltpu
from jax.sharding import Mesh, PartitionSpec as P

D = 5120
FF = 13824
NQ = 16
NT = 32
TOKX = 16
NTOK = 768

SIZES = (8, 2, 2, 4, 4)
NAMES = ("y", "zh", "core", "zl", "x")
BASIS = ("y", "zh", "core")
EX = ("zl", "x")
SWAP = ((0, 1), (1, 0))
bf16 = jnp.bfloat16
f32 = jnp.float32


def spread(x, axes, n):
    return lax.all_to_all(
        jnp.broadcast_to(x[None], (n,) + x.shape), axes, 0, 0, tiled=True
    )


def swap(x, axis):
    return lax.ppermute(x, axis, SWAP)


def tie(*values):
    return lax.optimization_barrier(values)


def ordered(mine, other, second):
    lo = jnp.where(second, other, mine)
    hi = jnp.where(second, mine, other)
    return lo, hi


def doubled(x, axis, bit):
    n = SIZES[NAMES.index(axis)]
    other = lax.ppermute(x, axis, [(i, i ^ bit) for i in range(n)])
    second = lax.axis_index(axis) // bit % 2 == 1
    return jnp.concatenate(ordered(x, other, second), axis=0)


def scattered(x, axis, dim):
    here = lax.axis_index(axis)
    total = lax.dynamic_index_in_dim(x, here, dim, keepdims=False)
    for bit in (1, 2, 3):
        block = lax.dynamic_index_in_dim(x, here ^ bit, dim, keepdims=False)
        total = total + lax.ppermute(block, axis, [(i, i ^ bit) for i in range(4)])
    return total


def summed(x, axis):
    one, two, three = (
        lax.ppermute(x, axis, [(i, i ^ bit) for i in range(4)]) for bit in (1, 2, 3)
    )
    return (x + one) + (two + three)


def score_kernel(grad_ref, act_ref, recip_ref, out_ref, grad_t, act_t, rows):
    first = NQ * TOKX
    grad_t[...] = grad_ref[first:, :].T
    act_t[...] = act_ref[first:, :].astype(f32).T

    def one_query(q, carry):
        here = pl.ds(pl.multiple_of(q * TOKX, TOKX), TOKX)
        outer = lax.dot_general(
            act_ref[here, :],
            grad_ref[here, :],
            (((0,), (0,)), ((), ())),
            preferred_element_type=f32,
        )
        precond = (outer * recip_ref[...]).astype(bf16)
        projected = jnp.dot(precond, grad_t[...], preferred_element_type=f32)
        rows[pl.ds(q, 1), :] = jnp.sum(projected * act_t[...], axis=0, keepdims=True)
        return carry

    lax.fori_loop(0, NQ, one_query, 0, unroll=2)

    slot = lax.broadcasted_iota(jnp.int32, (NT * TOKX, 128), 0)
    lane = lax.broadcasted_iota(jnp.int32, (NT * TOKX, 128), 1)
    pick = (slot // TOKX == lane % NT).astype(f32)
    sums = jnp.dot(
        rows[...], pick, preferred_element_type=f32, precision=lax.Precision.HIGHEST
    )
    query = lax.broadcasted_iota(jnp.int32, (NQ, 128), 0)
    place = lax.broadcasted_iota(jnp.int32, (NQ, 128), 1)
    sums = jnp.where(place // NT == query % 4, sums, 0.0)
    scale = TOKX * (float(FF) * float(D)) ** 0.5
    out_ref[...] = jnp.sum(sums.reshape(4, 4, 128), axis=1) / scale


def scores(rot_grad, rot_act, recip):
    cols_act, cols_grad = recip.shape
    vmem = pl.BlockSpec(memory_space=pltpu.VMEM)
    return pl.pallas_call(
        score_kernel,
        out_shape=jax.ShapeDtypeStruct((4, 128), f32),
        in_specs=[vmem] * 3,
        out_specs=vmem,
        scratch_shapes=[
            pltpu.VMEM((cols_grad, NT * TOKX), bf16),
            pltpu.VMEM((cols_act, NT * TOKX), f32),
            pltpu.VMEM((NQ, NT * TOKX), f32),
        ],
        compiler_params=pltpu.CompilerParams(vmem_limit_bytes=40 * 1024 * 1024),
        cost_estimate=pl.CostEstimate(
            flops=2 * NQ * cols_act * cols_grad * (NT * TOKX + TOKX),
            bytes_accessed=2 * NTOK * (cols_act + cols_grad) + 4 * cols_act * cols_grad,
            transcendentals=0,
        ),
    )(rot_grad, rot_act, recip)


def body(grad_out, acts, basis_out, basis_in, eigvals, counts):
    core = lax.axis_index("core")
    second = core == 1
    half = basis_out.shape[1] // 2

    grads = spread(grad_out, EX, 16).reshape(NTOK, -1)
    act = doubled(acts, "zh", 1)
    w_lo, w_hi = basis_out[:, :half], basis_out[:, half:]
    w_mine = jnp.where(second, w_hi, w_lo)
    w_other = swap(jnp.where(second, w_lo, w_hi), "core")
    b_other = swap(basis_in, "core")
    b_in = jnp.concatenate(ordered(basis_in, b_other, second), axis=1)
    act = doubled(act, "y", 1)
    act = doubled(act, "y", 2)
    grads, w_other, b_in, act = tie(grads, w_other, b_in, act)

    g_other = swap(grads, "core")
    partial = jnp.dot(grads, w_mine, preferred_element_type=f32)
    g_other, partial = tie(g_other, partial)
    partial = partial + jnp.dot(g_other, w_other, preferred_element_type=f32)
    partial, act = tie(partial.astype(bf16), act)

    rows = NTOK // 8
    pieces = lax.all_to_all(
        partial.reshape(8, rows, -1), "y", 0, 0, tiled=True
    )
    act = doubled(act, "y", 4)
    part_act = jnp.dot(act, b_in, preferred_element_type=f32)
    part_act = scattered(part_act.reshape(4, 4, 24, -1), "x", 1)
    eig_t = eigvals.T
    e_lo, e_hi = eig_t[:, :half], eig_t[:, half:]
    e_mine = jnp.where(second, e_hi, e_lo)
    e_other = swap(jnp.where(second, e_lo, e_hi), "core")
    slots = lax.axis_index("y") * rows + jnp.arange(rows, dtype=jnp.int32)
    used = slots % TOKX < jnp.take(counts, slots // TOKX)
    used = used.astype(f32)[:, None]
    pieces, part_act, used, e_other = tie(pieces, part_act, used, e_other)

    piece = jnp.sum(pieces.astype(f32), axis=0)
    piece_other = swap(piece, "zh")
    act_piece = summed(part_act, "zl").astype(bf16)
    piece = ((piece + piece_other) * used).astype(bf16)

    rot_grad = spread(piece, "y", 8).reshape(NTOK, -1)
    act_half = lax.all_gather(act_piece, "x", axis=0)
    act_half = jnp.swapaxes(act_half, 0, 1).reshape(16, 24, -1)
    act_other = swap(act_half, "core")
    rot_act = jnp.stack(ordered(act_half, act_other, second), axis=1).reshape(NTOK, -1)
    recip = 1.0 / jnp.concatenate(ordered(e_mine, e_other, second), axis=0)

    flat = scores(rot_grad, rot_act, recip)
    flat = jnp.sum(spread(flat, ("core",) + EX, 32), axis=0)
    flat = jnp.sum(spread(flat, ("y", "zh"), 16), axis=0)
    return flat.reshape(NQ, NT)


def solution(mesh):
    fine = Mesh(mesh.devices.reshape(SIZES), NAMES)
    return jax.shard_map(
        body,
        mesh=fine,
        in_specs=(
            P(EX, BASIS),
            P(BASIS, EX),
            P(BASIS, EX),
            P(EX, BASIS),
            P(EX, BASIS),
            P(),
        ),
        out_specs=P(),
        check_vma=False,
    )
```

```python
import jax
import jax.numpy as jnp
from jax import lax
from jax.experimental import pallas as pl
from jax.experimental.pallas import tpu as pltpu
from jax.sharding import Mesh, PartitionSpec as P

D = 5120
FF = 13824
NQ = 16
NT = 32
TOKX = 16
NTOK = 768

SIZES = (8, 2, 2, 4, 4)
NAMES = ("y", "zh", "core", "zl", "x")
BASIS = ("y", "zh", "core")
EX = ("zl", "x")
SWAP = ((0, 1), (1, 0))
bf16 = jnp.bfloat16
f32 = jnp.float32


def spread(x, axes, n):
    return lax.all_to_all(
        jnp.broadcast_to(x[None], (n,) + x.shape), axes, 0, 0, tiled=True
    )


def swap(x, axis):
    return lax.ppermute(x, axis, SWAP)


def tie(*values):
    return lax.optimization_barrier(values)


def padded(x, value):
    return jnp.pad(x, ((0, 0), (0, -x.shape[1] % 64)), constant_values=value)


def transposed_product(w, x):
    x = x.reshape(-1, x.shape[-1])
    return lax.dot_general(w, x, (((0,), (1,)), ((), ())), preferred_element_type=f32)


def ordered(mine, other, second):
    lo = jnp.where(second, other, mine)
    hi = jnp.where(second, mine, other)
    return lo, hi


def partner(x, axis, bit):
    n = SIZES[NAMES.index(axis)]
    return lax.ppermute(x, axis, [(i, i ^ bit) for i in range(n)])


def doubled(x, axis, bit):
    return jnp.concatenate([x, partner(x, axis, bit)], axis=0)


def input_kernel(x_ref, other_ref, w_ref, out_ref):
    n = x_ref.shape[0]
    out_ref[:n] = jnp.dot(x_ref[...], w_ref[...], preferred_element_type=f32)
    out_ref[n:] = jnp.dot(other_ref[...], w_ref[...], preferred_element_type=f32)


def input_product(x, other, w):
    x, other = (v.reshape(-1, v.shape[-1]) for v in (x, other))
    vmem = pl.BlockSpec(memory_space=pltpu.VMEM)
    return pl.pallas_call(
        input_kernel,
        out_shape=jax.ShapeDtypeStruct((2 * x.shape[0], w.shape[1]), f32),
        in_specs=[vmem] * 3,
        out_specs=vmem,
        compiler_params=pltpu.CompilerParams(vmem_limit_bytes=40 * 1024 * 1024),
        cost_estimate=pl.CostEstimate(
            flops=6000000000, bytes_accessed=8 * x.size, transcendentals=0
        ),
    )(x, other, w)


def scattered(x, axis, dim):
    here = lax.axis_index(axis)
    total = lax.dynamic_index_in_dim(x, here, dim, keepdims=False)
    for bit in (1, 2, 3):
        block = lax.dynamic_index_in_dim(x, here ^ bit, dim, keepdims=False)
        total = total + lax.ppermute(block, axis, [(i, i ^ bit) for i in range(4)])
    return total


def summed(x, axis):
    one, two, three = (
        lax.ppermute(x, axis, [(i, i ^ bit) for i in range(4)]) for bit in (1, 2, 3)
    )
    return (x + one) + (two + three)


def arrange_kernel(place_ref, half_ref, other_ref, query_ref, train_ref, act):
    here_yz, core = place_ref[0], place_ref[1]
    for block in range(NTOK // 48):
        far = here_yz ^ block
        zh, y1, y2, y4 = far & 1, (far >> 1) & 1, (far >> 2) & 1, (far >> 3) & 1
        at = 4 * (y4 + 2 * y2) + y1 + 2 * zh
        for ref, side in ((half_ref, core), (other_ref, 1 - core)):
            start = pl.multiple_of(48 * block + 24 * side, 8)
            act[pl.ds(start, 24), :] = ref[at].astype(f32)
    query_ref[...] = act[: NQ * TOKX, :].astype(bf16)
    train_ref[...] = act[NQ * TOKX :, :].T


def arranged(place, act_half, act_other):
    cols = act_half.shape[-1]
    vmem = pl.BlockSpec(memory_space=pltpu.VMEM)
    return pl.pallas_call(
        arrange_kernel,
        out_shape=(
            jax.ShapeDtypeStruct((NQ * TOKX, cols), bf16),
            jax.ShapeDtypeStruct((cols, NT * TOKX), f32),
        ),
        in_specs=[pl.BlockSpec(memory_space=pltpu.SMEM), vmem, vmem],
        out_specs=(vmem, vmem),
        scratch_shapes=[pltpu.VMEM((NTOK, cols), f32)],
        compiler_params=pltpu.CompilerParams(vmem_limit_bytes=40 * 1024 * 1024),
        cost_estimate=pl.CostEstimate(
            flops=5000000000, bytes_accessed=12 * NTOK * cols, transcendentals=0
        ),
    )(place, act_half, act_other)


def score_kernel(grad_ref, query_ref, train_ref, recip_ref, out_ref, grad_q, rows):
    grad_q[...] = grad_ref[:, : NQ * TOKX].T

    def one_query(q, carry):
        here = pl.ds(pl.multiple_of(q * TOKX, TOKX), TOKX)
        outer = lax.dot_general(
            query_ref[here, :],
            grad_q[here, :],
            (((0,), (0,)), ((), ())),
            preferred_element_type=f32,
        )
        precond = (outer * recip_ref[...]).astype(bf16)
        projected = jnp.dot(
            precond, grad_ref[:, NQ * TOKX :], preferred_element_type=f32
        )
        rows[pl.ds(q, 1), :] = jnp.sum(projected * train_ref[...], axis=0, keepdims=True)
        return carry

    lax.fori_loop(0, NQ, one_query, 0, unroll=2)

    slot = lax.broadcasted_iota(jnp.int32, (NT * TOKX, 128), 0)
    lane = lax.broadcasted_iota(jnp.int32, (NT * TOKX, 128), 1)
    pick = (slot // TOKX == lane % NT).astype(f32)
    sums = jnp.dot(
        rows[...], pick, preferred_element_type=f32, precision=lax.Precision.HIGHEST
    )
    query = lax.broadcasted_iota(jnp.int32, (NQ, 128), 0)
    place = lax.broadcasted_iota(jnp.int32, (NQ, 128), 1)
    sums = jnp.where(place // NT == query % 4, sums, 0.0)
    scale = TOKX * (float(FF) * float(D)) ** 0.5
    out_ref[...] = jnp.sum(sums.reshape(4, 4, 128), axis=1) / scale


def scores(rot_grad, query_act, train_act, recip):
    cols_act, cols_grad = recip.shape
    vmem = pl.BlockSpec(memory_space=pltpu.VMEM)
    return pl.pallas_call(
        score_kernel,
        out_shape=jax.ShapeDtypeStruct((4, 128), f32),
        in_specs=[vmem] * 4,
        out_specs=vmem,
        scratch_shapes=[
            pltpu.VMEM((NQ * TOKX, cols_grad), bf16),
            pltpu.VMEM((NQ, NT * TOKX), f32),
        ],
        compiler_params=pltpu.CompilerParams(vmem_limit_bytes=40 * 1024 * 1024),
        cost_estimate=pl.CostEstimate(
            flops=2 * NQ * cols_act * cols_grad * (NT * TOKX + TOKX),
            bytes_accessed=2 * NTOK * (cols_act + cols_grad) + 4 * cols_act * cols_grad,
            transcendentals=0,
        ),
    )(rot_grad, query_act, train_act, recip)


def body(grad_out, acts, basis_out, basis_in, eigvals, counts):
    core = lax.axis_index("core")
    second = core == 1
    half = basis_out.shape[1] // 2

    grads = spread(grad_out, EX, 16)
    act = doubled(acts[None], "y", 4)
    w_lo, w_hi = basis_out[:, :half], basis_out[:, half:]
    w_mine = padded(jnp.where(second, w_hi, w_lo), 0)
    w_other = swap(padded(jnp.where(second, w_lo, w_hi), 0), "core")
    b_other = swap(basis_in, "core")
    b_in = jnp.concatenate(ordered(basis_in, b_other, second), axis=1)
    act = doubled(act, "y", 2)
    act = doubled(act, "y", 1)
    grads, w_other, b_in, act = tie(grads, w_other, b_in, act)

    g_other = swap(grads, "core")
    partial = transposed_product(w_mine, grads)
    g_other, partial = tie(g_other, partial)
    partial = partial + transposed_product(w_other, g_other)
    partial = partial.astype(bf16)
    act_far = partner(act, "zh", 1)

    pieces = lax.all_to_all(
        partial.reshape(8, -1, NTOK), "y", 0, 0, tiled=True
    )
    product_act = input_product(act, act_far, b_in)
    eig_t = eigvals.T
    e_lo, e_hi = eig_t[:, :half], eig_t[:, half:]
    e_mine = jnp.where(second, e_hi, e_lo)
    e_send = jnp.where(second, e_lo, e_hi)
    e_send, in_use, product_act = tie(e_send, counts, product_act)
    e_other = swap(e_send, "core")
    part_act = scattered(product_act.reshape(4, 4, 24, -1), "x", 1)
    slots = lax.broadcasted_iota(jnp.int32, (NQ + NT, TOKX), 1)
    used = (slots < in_use[:, None]).astype(f32).reshape(1, NTOK)
    pieces, part_act, used, e_other = tie(pieces, part_act, used, e_other)

    piece = jnp.sum(pieces.astype(f32), axis=0)
    piece_other = swap(piece, "zh")
    act_piece = summed(part_act, "zl").astype(bf16)
    piece = ((piece + piece_other) * used).astype(bf16)

    rot_grad = spread(piece, "y", 8).reshape(-1, NTOK)
    act_half = lax.all_gather(act_piece, "x", axis=0)
    act_half = act_half.reshape(16, 24, -1)
    act_other = swap(act_half, "core")
    recip = 1.0 / jnp.concatenate(ordered(e_mine, e_other, second), axis=0)
    recip = padded(recip, 1)

    place = jnp.stack([2 * lax.axis_index("y") + lax.axis_index("zh"), core])
    query_act, train_act = arranged(place, act_half, act_other)
    flat = scores(rot_grad, query_act, train_act, recip)
    flat = jnp.sum(spread(flat, ("core",) + EX, 32), axis=0)
    flat = jnp.sum(spread(flat, ("y", "zh"), 16), axis=0)
    return flat.reshape(NQ, NT)


def solution(mesh):
    fine = Mesh(mesh.devices.reshape(SIZES), NAMES)
    return jax.shard_map(
        body,
        mesh=fine,
        in_specs=(
            P(EX, BASIS),
            P(BASIS, EX),
            P(BASIS, EX),
            P(EX, BASIS),
            P(EX, BASIS),
            P(),
        ),
        out_specs=P(),
        check_vma=False,
    )
```

```python
import jax
import jax.numpy as jnp
from jax import lax
from jax.experimental import pallas as pl
from jax.experimental.pallas import tpu as pltpu
from jax.sharding import Mesh, PartitionSpec as P

D = 5120
FF = 13824
NQ = 16
NT = 32
TOKX = 16
NTOK = 768

SIZES = (8, 2, 2, 4, 4)
NAMES = ("y", "zh", "core", "zl", "x")
BASIS = ("y", "zh", "core")
EX = ("zl", "x")
SWAP = ((0, 1), (1, 0))
bf16 = jnp.bfloat16
f32 = jnp.float32


def spread(x, axes, n):
    return lax.all_to_all(
        jnp.broadcast_to(x[None], (n,) + x.shape), axes, 0, 0, tiled=True
    )


def swap(x, axis):
    return lax.ppermute(x, axis, SWAP)


def tie(*values):
    return lax.optimization_barrier(values)


def padded(x, value):
    return jnp.pad(x, ((0, 0), (0, -x.shape[1] % 64)), constant_values=value)


def transposed_product(w, x):
    x = x.reshape(-1, x.shape[-1])
    return lax.dot_general(w, x, (((0,), (1,)), ((), ())), preferred_element_type=f32)


def ordered(mine, other, second):
    lo = jnp.where(second, other, mine)
    hi = jnp.where(second, mine, other)
    return lo, hi


def partner(x, axis, bit):
    n = SIZES[NAMES.index(axis)]
    return lax.ppermute(x, axis, [(i, i ^ bit) for i in range(n)])


def doubled(x, axis, bit):
    return jnp.concatenate([x, partner(x, axis, bit)], axis=0)


def input_kernel(x_ref, other_ref, w_ref, out_ref):
    n = x_ref.shape[0]
    out_ref[:n] = jnp.dot(x_ref[...], w_ref[...], preferred_element_type=f32)
    out_ref[n:] = jnp.dot(other_ref[...], w_ref[...], preferred_element_type=f32)


def input_product(x, other, w):
    x, other = (v.reshape(-1, v.shape[-1]) for v in (x, other))
    vmem = pl.BlockSpec(memory_space=pltpu.VMEM)
    return pl.pallas_call(
        input_kernel,
        out_shape=jax.ShapeDtypeStruct((2 * x.shape[0], w.shape[1]), f32),
        in_specs=[vmem] * 3,
        out_specs=vmem,
        compiler_params=pltpu.CompilerParams(vmem_limit_bytes=40 * 1024 * 1024),
        cost_estimate=pl.CostEstimate(
            flops=6000000000, bytes_accessed=8 * x.size, transcendentals=0
        ),
    )(x, other, w)


def scattered(x, axis, dim):
    here = lax.axis_index(axis)
    total = lax.dynamic_index_in_dim(x, here, dim, keepdims=False)
    for bit in (1, 2, 3):
        block = lax.dynamic_index_in_dim(x, here ^ bit, dim, keepdims=False)
        total = total + lax.ppermute(block, axis, [(i, i ^ bit) for i in range(4)])
    return total


def summed(x, axis):
    one, two, three = (
        lax.ppermute(x, axis, [(i, i ^ bit) for i in range(4)]) for bit in (1, 2, 3)
    )
    return (x + one) + (two + three)


def arrange_kernel(place_ref, half_ref, other_ref, query_ref, train_ref, act):
    here_yz, core = place_ref[0], place_ref[1]
    for block in range(NTOK // 48):
        far = here_yz ^ block
        zh, y1, y2, y4 = far & 1, (far >> 1) & 1, (far >> 2) & 1, (far >> 3) & 1
        at = 4 * (y4 + 2 * y2) + y1 + 2 * zh
        for ref, side in ((half_ref, core), (other_ref, 1 - core)):
            start = pl.multiple_of(48 * block + 24 * side, 8)
            act[pl.ds(start, 24), :] = ref[at].astype(f32)
    query_ref[...] = act[: NQ * TOKX, :].astype(bf16)
    train_ref[...] = act[NQ * TOKX :, :].T


def arranged(place, act_half, act_other):
    cols = act_half.shape[-1]
    vmem = pl.BlockSpec(memory_space=pltpu.VMEM)
    return pl.pallas_call(
        arrange_kernel,
        out_shape=(
            jax.ShapeDtypeStruct((NQ * TOKX, cols), bf16),
            jax.ShapeDtypeStruct((cols, NT * TOKX), f32),
        ),
        in_specs=[pl.BlockSpec(memory_space=pltpu.SMEM), vmem, vmem],
        out_specs=(vmem, vmem),
        scratch_shapes=[pltpu.VMEM((NTOK, cols), f32)],
        compiler_params=pltpu.CompilerParams(vmem_limit_bytes=40 * 1024 * 1024),
        cost_estimate=pl.CostEstimate(
            flops=5000000000, bytes_accessed=12 * NTOK * cols, transcendentals=0
        ),
    )(place, act_half, act_other)


def score_kernel(grad_ref, query_ref, train_ref, recip_ref, out_ref, grad_q, rows):
    grad_q[...] = grad_ref[:, : NQ * TOKX].T

    def one_query(q, carry):
        here = pl.ds(pl.multiple_of(q * TOKX, TOKX), TOKX)
        outer = lax.dot_general(
            query_ref[here, :],
            grad_q[here, :],
            (((0,), (0,)), ((), ())),
            preferred_element_type=f32,
        )
        precond = (outer * recip_ref[...]).astype(bf16)
        projected = jnp.dot(
            precond, grad_ref[:, NQ * TOKX :], preferred_element_type=f32
        )
        rows[pl.ds(q, 1), :] = jnp.sum(projected * train_ref[...], axis=0, keepdims=True)
        return carry

    lax.fori_loop(0, NQ, one_query, 0, unroll=16)

    slot = lax.broadcasted_iota(jnp.int32, (NT * TOKX, 128), 0)
    lane = lax.broadcasted_iota(jnp.int32, (NT * TOKX, 128), 1)
    pick = (slot // TOKX == lane % NT).astype(f32)
    sums = jnp.dot(
        rows[...], pick, preferred_element_type=f32, precision=lax.Precision.HIGHEST
    )
    query = lax.broadcasted_iota(jnp.int32, (NQ, 128), 0)
    place = lax.broadcasted_iota(jnp.int32, (NQ, 128), 1)
    sums = jnp.where(place // NT == query % 4, sums, 0.0)
    scale = TOKX * (float(FF) * float(D)) ** 0.5
    out_ref[...] = jnp.sum(sums.reshape(4, 4, 128), axis=1) / scale


def scores(rot_grad, query_act, train_act, recip):
    cols_act, cols_grad = recip.shape
    vmem = pl.BlockSpec(memory_space=pltpu.VMEM)
    return pl.pallas_call(
        score_kernel,
        out_shape=jax.ShapeDtypeStruct((4, 128), f32),
        in_specs=[vmem] * 4,
        out_specs=vmem,
        scratch_shapes=[
            pltpu.VMEM((NQ * TOKX, cols_grad), bf16),
            pltpu.VMEM((NQ, NT * TOKX), f32),
        ],
        compiler_params=pltpu.CompilerParams(vmem_limit_bytes=40 * 1024 * 1024),
        cost_estimate=pl.CostEstimate(
            flops=2 * NQ * cols_act * cols_grad * (NT * TOKX + TOKX),
            bytes_accessed=2 * NTOK * (cols_act + cols_grad) + 4 * cols_act * cols_grad,
            transcendentals=0,
        ),
    )(rot_grad, query_act, train_act, recip)


def body(grad_out, acts, basis_out, basis_in, eigvals, counts):
    core = lax.axis_index("core")
    second = core == 1
    half = basis_out.shape[1] // 2

    grads = spread(grad_out, EX, 16)
    act = doubled(acts[None], "y", 4)
    w_lo, w_hi = basis_out[:, :half], basis_out[:, half:]
    w_mine = padded(jnp.where(second, w_hi, w_lo), 0)
    w_other = swap(padded(jnp.where(second, w_lo, w_hi), 0), "core")
    b_other = swap(basis_in, "core")
    b_in = jnp.concatenate(ordered(basis_in, b_other, second), axis=1)
    act = doubled(act, "y", 2)
    act = doubled(act, "y", 1)
    grads, w_other, b_in, act = tie(grads, w_other, b_in, act)

    g_other = swap(grads, "core")
    partial = transposed_product(w_mine, grads)
    g_other, partial = tie(g_other, partial)
    partial = partial + transposed_product(w_other, g_other)
    partial = partial.astype(bf16)
    act_far = partner(act, "zh", 1)

    pieces = lax.all_to_all(
        partial.reshape(8, -1, NTOK), "y", 0, 0, tiled=True
    )
    product_act = input_product(act, act_far, b_in)
    eig_t = eigvals.T
    e_lo, e_hi = eig_t[:, :half], eig_t[:, half:]
    e_mine = jnp.where(second, e_hi, e_lo)
    e_send = jnp.where(second, e_lo, e_hi)
    e_send, in_use, product_act = tie(e_send, counts, product_act)
    e_other = swap(e_send, "core")
    part_act = scattered(product_act.reshape(4, 4, 24, -1), "x", 1)
    slots = lax.broadcasted_iota(jnp.int32, (NQ + NT, TOKX), 1)
    used = (slots < in_use[:, None]).astype(f32).reshape(1, NTOK)
    pieces, part_act, used, e_other = tie(pieces, part_act, used, e_other)

    piece = jnp.sum(pieces.astype(f32), axis=0)
    piece_other = swap(piece, "zh")
    act_piece = summed(part_act, "zl").astype(bf16)
    piece = ((piece + piece_other) * used).astype(bf16)

    rot_grad = spread(piece, "y", 8).reshape(-1, NTOK)
    act_half = lax.all_gather(act_piece, "x", axis=0)
    act_half = act_half.reshape(16, 24, -1)
    act_other = swap(act_half, "core")
    recip = 1.0 / jnp.concatenate(ordered(e_mine, e_other, second), axis=0)
    recip = padded(recip, 1)

    place = jnp.stack([2 * lax.axis_index("y") + lax.axis_index("zh"), core])
    query_act, train_act = arranged(place, act_half, act_other)
    flat = scores(rot_grad, query_act, train_act, recip)
    flat = jnp.sum(spread(flat, ("core",) + EX, 32), axis=0)
    flat = jnp.sum(spread(flat, ("y", "zh"), 16), axis=0)
    return flat.reshape(NQ, NT)


def solution(mesh):
    fine = Mesh(mesh.devices.reshape(SIZES), NAMES)
    return jax.shard_map(
        body,
        mesh=fine,
        in_specs=(
            P(EX, BASIS),
            P(BASIS, EX),
            P(BASIS, EX),
            P(EX, BASIS),
            P(EX, BASIS),
            P(),
        ),
        out_specs=P(),
        check_vma=False,
    )
```

```python
import jax
import jax.numpy as jnp
from jax import lax
from jax.experimental import pallas as pl
from jax.experimental.pallas import tpu as pltpu
from jax.sharding import Mesh, PartitionSpec as P

D = 5120
FF = 13824
NQ = 16
NT = 32
TOKX = 16
NTOK = 768

SIZES = (8, 2, 2, 4, 4)
NAMES = ("y", "zh", "core", "zl", "x")
BASIS = ("y", "zh", "core")
EX = ("zl", "x")
SWAP = ((0, 1), (1, 0))
bf16 = jnp.bfloat16
f32 = jnp.float32


def spread(x, axes, n):
    return lax.all_to_all(
        jnp.broadcast_to(x[None], (n,) + x.shape), axes, 0, 0, tiled=True
    )


def swap(x, axis):
    return lax.ppermute(x, axis, SWAP)


def tie(*values):
    return lax.optimization_barrier(values)


def padded(x, value):
    return jnp.pad(x, ((0, 0), (0, -x.shape[1] % 64)), constant_values=value)


def transposed_product(w, x):
    x = x.reshape(-1, x.shape[-1])
    return lax.dot_general(w, x, (((0,), (1,)), ((), ())), preferred_element_type=f32)


def ordered(mine, other, second):
    lo = jnp.where(second, other, mine)
    hi = jnp.where(second, mine, other)
    return lo, hi


def partner(x, axis, bit):
    n = SIZES[NAMES.index(axis)]
    return lax.ppermute(x, axis, [(i, i ^ bit) for i in range(n)])


def doubled(x, axis, bit):
    return jnp.concatenate([x, partner(x, axis, bit)], axis=0)


def input_kernel(x_ref, other_ref, w_ref, out_ref):
    n = x_ref.shape[0]
    out_ref[:n] = jnp.dot(x_ref[...], w_ref[...], preferred_element_type=f32)
    out_ref[n:] = jnp.dot(other_ref[...], w_ref[...], preferred_element_type=f32)


def input_product(x, other, w):
    x, other = (v.reshape(-1, v.shape[-1]) for v in (x, other))
    vmem = pl.BlockSpec(memory_space=pltpu.VMEM)
    return pl.pallas_call(
        input_kernel,
        out_shape=jax.ShapeDtypeStruct((2 * x.shape[0], w.shape[1]), f32),
        in_specs=[vmem] * 3,
        out_specs=vmem,
        compiler_params=pltpu.CompilerParams(vmem_limit_bytes=40 * 1024 * 1024),
        cost_estimate=pl.CostEstimate(
            flops=6000000000, bytes_accessed=8 * x.size, transcendentals=0
        ),
    )(x, other, w)


def scattered(x, axis, dim):
    here = lax.axis_index(axis)
    total = lax.dynamic_index_in_dim(x, here, dim, keepdims=False)
    for bit in (1, 2, 3):
        block = lax.dynamic_index_in_dim(x, here ^ bit, dim, keepdims=False)
        total = total + lax.ppermute(block, axis, [(i, i ^ bit) for i in range(4)])
    return total


def summed(x, axis):
    one, two, three = (
        lax.ppermute(x, axis, [(i, i ^ bit) for i in range(4)]) for bit in (1, 2, 3)
    )
    return (x + one) + (two + three)


def arrange_kernel(place_ref, half_ref, other_ref, query_ref, train_ref, act):
    here_yz, core = place_ref[0], place_ref[1]
    for block in range(NTOK // 48):
        far = here_yz ^ block
        zh, y1, y2, y4 = far & 1, (far >> 1) & 1, (far >> 2) & 1, (far >> 3) & 1
        at = 4 * (y4 + 2 * y2) + y1 + 2 * zh
        for ref, side in ((half_ref, core), (other_ref, 1 - core)):
            start = pl.multiple_of(48 * block + 24 * side, 8)
            act[pl.ds(start, 24), :] = ref[at].astype(f32)
    query_ref[...] = act[: NQ * TOKX, :].astype(bf16)
    train_ref[...] = act[NQ * TOKX :, :].T


def arranged(place, act_half, act_other):
    cols = act_half.shape[-1]
    vmem = pl.BlockSpec(memory_space=pltpu.VMEM)
    return pl.pallas_call(
        arrange_kernel,
        out_shape=(
            jax.ShapeDtypeStruct((NQ * TOKX, cols), bf16),
            jax.ShapeDtypeStruct((cols, NT * TOKX), f32),
        ),
        in_specs=[pl.BlockSpec(memory_space=pltpu.SMEM), vmem, vmem],
        out_specs=(vmem, vmem),
        scratch_shapes=[pltpu.VMEM((NTOK, cols), f32)],
        compiler_params=pltpu.CompilerParams(vmem_limit_bytes=40 * 1024 * 1024),
        cost_estimate=pl.CostEstimate(
            flops=5000000000, bytes_accessed=12 * NTOK * cols, transcendentals=0
        ),
    )(place, act_half, act_other)


def score_kernel(grad_ref, query_ref, train_ref, recip_ref, out_ref, grad_q, rows):
    grad_q[...] = grad_ref[:, : NQ * TOKX].T

    def one_query(q, carry):
        here = pl.ds(pl.multiple_of(q * TOKX, TOKX), TOKX)
        outer = lax.dot_general(
            query_ref[here, :],
            grad_q[here, :],
            (((0,), (0,)), ((), ())),
            preferred_element_type=f32,
        )
        precond = (outer * recip_ref[...]).astype(bf16)
        projected = jnp.dot(
            precond, grad_ref[:, NQ * TOKX :], preferred_element_type=f32
        )
        rows[pl.ds(q, 1), :] = jnp.sum(projected * train_ref[...], axis=0, keepdims=True)
        return carry

    lax.fori_loop(0, NQ, one_query, 0, unroll=16)

    slot = lax.broadcasted_iota(jnp.int32, (NT * TOKX, 128), 0)
    lane = lax.broadcasted_iota(jnp.int32, (NT * TOKX, 128), 1)
    pick = (slot // TOKX == lane % NT).astype(f32)
    sums = jnp.dot(
        rows[...], pick, preferred_element_type=f32, precision=lax.Precision.HIGHEST
    )
    query = lax.broadcasted_iota(jnp.int32, (NQ, 128), 0)
    place = lax.broadcasted_iota(jnp.int32, (NQ, 128), 1)
    sums = jnp.where(place // NT == query % 4, sums, 0.0)
    scale = TOKX * (float(FF) * float(D)) ** 0.5
    out_ref[...] = jnp.sum(sums.reshape(4, 4, 128), axis=1) / scale


def scores(rot_grad, query_act, train_act, recip):
    cols_act, cols_grad = recip.shape
    vmem = pl.BlockSpec(memory_space=pltpu.VMEM)
    return pl.pallas_call(
        score_kernel,
        out_shape=jax.ShapeDtypeStruct((4, 128), f32),
        in_specs=[vmem] * 4,
        out_specs=vmem,
        scratch_shapes=[
            pltpu.VMEM((NQ * TOKX, cols_grad), bf16),
            pltpu.VMEM((NQ, NT * TOKX), f32),
        ],
        compiler_params=pltpu.CompilerParams(vmem_limit_bytes=40 * 1024 * 1024),
        cost_estimate=pl.CostEstimate(
            flops=2 * NQ * cols_act * cols_grad * (NT * TOKX + TOKX),
            bytes_accessed=2 * NTOK * (cols_act + cols_grad) + 4 * cols_act * cols_grad,
            transcendentals=0,
        ),
    )(rot_grad, query_act, train_act, recip)


def body(grad_out, acts, basis_out, basis_in, eigvals, counts):
    core = lax.axis_index("core")
    second = core == 1
    half = basis_out.shape[1] // 2

    grads = spread(grad_out, EX, 16)
    act = doubled(acts[None], "y", 4)
    w_lo, w_hi = basis_out[:, :half], basis_out[:, half:]
    w_mine = padded(jnp.where(second, w_hi, w_lo), 0)
    w_other = swap(padded(jnp.where(second, w_lo, w_hi), 0), "core")
    b_other = swap(basis_in, "core")
    b_in = jnp.concatenate(ordered(basis_in, b_other, second), axis=1)
    act = doubled(act, "y", 2)
    act = doubled(act, "y", 1)
    grads, w_other, b_in, act = tie(grads, w_other, b_in, act)

    g_other = swap(grads, "core")
    partial = transposed_product(w_mine, grads)
    g_other, partial = tie(g_other, partial)
    partial = partial + transposed_product(w_other, g_other)
    partial = partial.astype(bf16)
    act_far = partner(act, "zh", 1)

    pieces = lax.all_to_all(
        partial.reshape(8, -1, NTOK), "y", 0, 0, tiled=True
    )
    product_act = input_product(act, act_far, b_in)
    eig_t = eigvals.T
    e_lo, e_hi = eig_t[:, :half], eig_t[:, half:]
    e_mine = jnp.where(second, e_hi, e_lo)
    e_send = jnp.where(second, e_lo, e_hi)
    e_send, in_use, product_act = tie(e_send, counts, product_act)
    e_other = swap(e_send, "core")
    part_act = scattered(product_act.reshape(4, 4, 24, -1), "x", 1)
    slots = lax.broadcasted_iota(jnp.int32, (NQ + NT, TOKX), 1)
    used = (slots < in_use[:, None]).astype(f32).reshape(1, NTOK)
    pieces, part_act, used, e_other = tie(pieces, part_act, used, e_other)

    piece = jnp.sum(pieces.astype(f32), axis=0)
    piece_other = swap(piece.astype(bf16), "zh").astype(f32)
    act_piece = summed(part_act, "zl").astype(bf16)
    piece = ((piece + piece_other) * used).astype(bf16)

    rot_grad = spread(piece, "y", 8).reshape(-1, NTOK)
    act_half = lax.all_gather(act_piece, "x", axis=0)
    act_half = act_half.reshape(16, 24, -1)
    act_other = swap(act_half, "core")
    recip = 1.0 / jnp.concatenate(ordered(e_mine, e_other, second), axis=0)
    recip = padded(recip, 1)

    place = jnp.stack([2 * lax.axis_index("y") + lax.axis_index("zh"), core])
    query_act, train_act = arranged(place, act_half, act_other)
    flat = scores(rot_grad, query_act, train_act, recip)
    flat = jnp.sum(spread(flat, ("core",) + EX, 32), axis=0)
    flat = jnp.sum(spread(flat, ("y", "zh"), 16), axis=0)
    return flat.reshape(NQ, NT)


def solution(mesh):
    fine = Mesh(mesh.devices.reshape(SIZES), NAMES)
    return jax.shard_map(
        body,
        mesh=fine,
        in_specs=(
            P(EX, BASIS),
            P(BASIS, EX),
            P(BASIS, EX),
            P(EX, BASIS),
            P(EX, BASIS),
            P(),
        ),
        out_specs=P(),
        check_vma=False,
    )
```
